32 devices in a mesh: dp: 8 (over z, y), mp: 4 (over x, core).
Axes of the slice: x: 2, y: 2, z: 4, core: 2. Of those that a mesh axis runs over, the one named last changes fastest.
Arguments:
- latent: bfloat16 [4096, 512], P('dp', 'mp'), may hold values from -6 to 6
- action: bfloat16 [4096, 6], P('dp'), may hold values from -1 to 1
- task_ids: int32 [4096], P('dp'), may hold values from 0 to 79
- action_mask: int32 [80, 6], replicated, may hold values 0 or 1
- cotangent: bfloat16 [4096, 512], P('dp', 'mp'), may hold values from -6 to 6
- task_table: float32 [80, 96], replicated, may hold values from -6 to 6
- lat_weight: float32 [512, 1024], P('dp', 'mp'), may hold values from -0.25 to 0.25
- act_weight: float32 [6, 1024], replicated, may hold values from -2.5 to 2.5
- task_weight: float32 [96, 1024], replicated, may hold values from -0.625 to 0.625
- bias_one: float32 [1024], replicated, may hold values from -3 to 3
- gain_one: float32 [1024], replicated, may hold values from 0.25 to 1.75
- shift_one: float32 [1024], replicated, may hold values from -3 to 3
- hid_weight: float32 [1024, 1024], P('mp', 'dp'), may hold values from -0.1875 to 0.1875
- bias_two: float32 [1024], replicated, may hold values from -3 to 3
- gain_two: float32 [1024], replicated, may hold values from 0.25 to 1.75
- shift_two: float32 [1024], replicated, may hold values from -3 to 3
- out_weight: float32 [1024, 512], P('dp', 'mp'), may hold values from -0.375 to 0.375
- bias_three: float32 [512], replicated, may hold values from -4 to 4
- gain_three: float32 [512], replicated, may hold values from 0.25 to 1.75
- shift_three: float32 [512], replicated, may hold values from -3 to 3
Outputs:
- next_latent: bfloat16 [4096, 512], P('dp', 'mp')
- latent_grad: bfloat16 [4096, 512], P('dp', 'mp')
- table_grad: float32 [80, 96], replicated
- lat_weight_grad: float32 [512, 1024], P('dp', 'mp')
- act_weight_grad: float32 [6, 1024], replicated
- task_weight_grad: float32 [96, 1024], replicated
- bias_one_grad: float32 [1024], replicated
- gain_one_grad: float32 [1024], replicated
- shift_one_grad: float32 [1024], replicated
- hid_weight_grad: float32 [1024, 1024], P('mp', 'dp')
- bias_two_grad: float32 [1024], replicated
- gain_two_grad: float32 [1024], replicated
- shift_two_grad: float32 [1024], replicated
- out_weight_grad: float32 [1024, 512], P('dp', 'mp')
- bias_three_grad: float32 [512], replicated
- gain_three_grad: float32 [512], replicated
- shift_three_grad: float32 [512], replicated
The draws below stay inside these ranges and needn't reach their ends.
All inputs are finite; a program needn't handle non-finite values.
Results may differ from the reference program's by a relative error of at most 0.012.
Values may be sent and summed in bfloat16 or wider, within the bound.
No kernel may reach another device: no remote copies, remote signals or barrier semaphores. Data moves between devices by JAX's collectives and lax.ppermute only.
A program may use at most 64 MiB of HBM per device.

```python
import jax
import jax.numpy as jnp
from jax import lax

LAT = 512
HID = 1024
ACT = 6
TDIM = 96
TASKS = 80
GROUP = 8
ROWS = 4096


def touch_ends(array, rng, least, largest):
    spot = [jax.random.randint(jax.random.fold_in(rng, axis), (), 0, length) for axis, length in enumerate(array.shape)]
    longest = array.shape.index(max(array.shape))
    beside = spot[:longest] + [(spot[longest] + 1) % array.shape[longest]] + spot[longest + 1:]
    return array.at[tuple(spot)].set(least).at[tuple(beside)].set(largest)


def level_of(stream_key, extent, cuts, low, largest):
    level = 1.0
    for dim, blocks in cuts:
        steps = jax.random.uniform(jax.random.fold_in(jax.random.fold_in(stream_key, 6), dim), (blocks,), jnp.float32, low / len(cuts), largest / len(cuts))
        level = level * jnp.repeat(jnp.exp(steps), extent[dim] // blocks).reshape((-1,) + (1,) * (len(extent) - 1 - dim))
    return level


def noise(stream_key, dims, deviation, limit, cuts=(), kind=jnp.bfloat16):
    level = level_of(stream_key, dims, cuts, -0.22, 0.18) if cuts else 1.0
    entries = jax.random.normal(stream_key, dims, jnp.float32) * deviation * level
    return jnp.minimum(jnp.maximum(entries, -limit), limit).astype(kind)


def setup_inputs(seed: int = 0) -> dict:
    arg_keys = jax.random.split(jax.random.key(seed), 21)
    latent = noise(arg_keys[0], (ROWS, LAT), 1.0, 6.0, ((0, 8), (1, 4)))
    action = jnp.clip(jax.random.uniform(arg_keys[1], (ROWS, ACT), jnp.float32, -1.0, 1.0) * level_of(arg_keys[1], (ROWS, ACT), ((0, 8),), -0.4, 0.0), -1.0, 1.0).astype(jnp.bfloat16)
    task_ids = touch_ends(jax.random.randint(arg_keys[2], (ROWS,), 0, TASKS), jax.random.fold_in(arg_keys[2], 1), 0, TASKS - 1).astype(jnp.int32)
    action_mask = touch_ends((jax.random.randint(arg_keys[3], (TASKS, ACT), 0, 3) < 2).astype(jnp.int32), jax.random.fold_in(arg_keys[3], 1), 0, 1)
    cotangent = noise(arg_keys[4], (ROWS, LAT), 1.0, 6.0, ((0, 8), (1, 4)))
    task_table = noise(arg_keys[5], (TASKS, TDIM), 1.0, 6.0, (), jnp.float32)
    lat_weight = noise(arg_keys[6], (LAT, HID), LAT ** -0.5, 0.25, ((0, 8), (1, 4)), jnp.float32)
    act_weight = noise(arg_keys[7], (ACT, HID), ACT ** -0.5, 2.5, (), jnp.float32)
    task_weight = noise(arg_keys[8], (TDIM, HID), TDIM ** -0.5, 0.625, (), jnp.float32)
    bias_one = noise(arg_keys[9], (HID,), 0.5, 3.0, (), jnp.float32)
    gain_one = jnp.clip(1.0 + 0.15 * jax.random.normal(arg_keys[10], (HID,), jnp.float32), 0.25, 1.75)
    shift_one = noise(arg_keys[11], (HID,), 0.5, 3.0, (), jnp.float32)
    hid_weight = noise(arg_keys[12], (HID, HID), HID ** -0.5, 0.1875, ((0, 4), (1, 8)), jnp.float32)
    bias_two = noise(arg_keys[13], (HID,), 0.5, 3.0, (), jnp.float32)
    gain_two = jnp.clip(1.0 + 0.15 * jax.random.normal(arg_keys[14], (HID,), jnp.float32), 0.25, 1.75)
    shift_two = noise(arg_keys[15], (HID,), 0.5, 3.0, (), jnp.float32)
    out_weight = noise(arg_keys[16], (HID, LAT), (HID // 4) ** -0.5, 0.375, ((0, 8), (1, 4)), jnp.float32)
    bias_three = noise(arg_keys[17], (LAT,), 1.0, 4.0, (), jnp.float32)
    gain_three = jnp.clip(1.0 + 0.15 * jax.random.normal(arg_keys[18], (LAT,), jnp.float32), 0.25, 1.75)
    shift_three = noise(arg_keys[19], (LAT,), 0.5, 3.0, (), jnp.float32)
    return {"latent": latent, "action": action, "task_ids": task_ids, "action_mask": action_mask, "cotangent": cotangent, "task_table": task_table, "lat_weight": lat_weight, "act_weight": act_weight, "task_weight": task_weight, "bias_one": bias_one, "gain_one": gain_one, "shift_one": shift_one, "hid_weight": hid_weight, "bias_two": bias_two, "gain_two": gain_two, "shift_two": shift_two, "out_weight": out_weight, "bias_three": bias_three, "gain_three": gain_three, "shift_three": shift_three}


EPS = 1e-05

@jax.custom_vjp
def low(v):
    return lax.optimization_barrier(v.astype(jnp.bfloat16)).astype(jnp.float32)

@jax.custom_vjp
def low_back(v):
    return v

def low_keep(v):
    return (low(v), None)

def low_pass(kept, grad):
    return (grad,)

def back_keep(v):
    return (v, None)

def back_low(kept, grad):
    return (low(grad),)
low.defvjp(low_keep, low_pass)
low_back.defvjp(back_keep, back_low)

def matmul(left, right):
    return jnp.dot(left, right, precision=lax.Precision.HIGHEST, preferred_element_type=jnp.float32)

def mish(value):
    return value * jnp.tanh(jax.nn.softplus(value))

def layer_norm(hidden, gain, shift):
    center = lax.optimization_barrier(jnp.mean(hidden, axis=-1, keepdims=True))
    spread = lax.optimization_barrier(jnp.mean(hidden * hidden, axis=-1, keepdims=True)) - center * center
    return (hidden - center) * lax.rsqrt(spread + EPS) * gain + shift

def simplex_norm(hidden):
    grouped = hidden.reshape(hidden.shape[0], -1, GROUP)
    return jax.nn.softmax(grouped, axis=-1).reshape(hidden.shape)

def forward(onehot, moves, latent, task_table, lat_weight, act_weight, task_weight, bias_one, gain_one, shift_one, hid_weight, bias_two, gain_two, shift_two, out_weight, bias_three, gain_three, shift_three):
    task_vec = matmul(onehot, task_table)
    first = matmul(low(latent), low(lat_weight)) + matmul(low(moves), low(act_weight)) + matmul(low(task_vec), low(task_weight)) + bias_one
    first = low_back(first)
    active_one = low(mish(layer_norm(first, gain_one, shift_one)))
    second = low_back(matmul(active_one, low(hid_weight)) + bias_two)
    active_two = low(mish(layer_norm(second, gain_two, shift_two)))
    third = low_back(matmul(active_two, low(out_weight)) + bias_three)
    return simplex_norm(layer_norm(third, gain_three, shift_three))

def reference(latent, action, task_ids, action_mask, cotangent, task_table, lat_weight, act_weight, task_weight, bias_one, gain_one, shift_one, hid_weight, bias_two, gain_two, shift_two, out_weight, bias_three, gain_three, shift_three):
    params = (task_table, lat_weight, act_weight, task_weight, bias_one, gain_one, shift_one, hid_weight, bias_two, gain_two, shift_two, out_weight, bias_three, gain_three, shift_three)
    block = min(4096, ROWS)
    count = ROWS // block
    lat_blocks = latent.reshape(count, block, LAT)
    act_blocks = action.reshape(count, block, ACT)
    ids_blocks = task_ids.reshape(count, block)
    cot_blocks = cotangent.reshape(count, block, LAT)
    mask_float = action_mask.astype(jnp.float32)

    def step(totals, pieces):
        lat_piece, act_piece, ids_piece, cot_piece = pieces
        onehot = (ids_piece[:, None] == jnp.arange(TASKS, dtype=jnp.int32)[None, :]).astype(jnp.float32)
        moves = act_piece.astype(jnp.float32) * matmul(onehot, mask_float)

        def local(latent_in, *weights):
            return forward(onehot, moves, latent_in, *weights)
        result, pullback = jax.vjp(local, lat_piece.astype(jnp.float32), *params)
        grads = pullback(cot_piece.astype(jnp.float32))
        totals = tuple((total + grad for total, grad in zip(totals, grads[1:])))
        return (totals, (result.astype(jnp.bfloat16), grads[0].astype(jnp.bfloat16)))
    start = tuple((jnp.zeros(p.shape, jnp.float32) for p in params))
    totals, outputs = lax.scan(step, start, (lat_blocks, act_blocks, ids_blocks, cot_blocks))
    next_latent = outputs[0].reshape(ROWS, LAT)
    latent_grad = outputs[1].reshape(ROWS, LAT)
    return (next_latent, latent_grad, totals[0], totals[1], totals[2], totals[3], totals[4], totals[5], totals[6], totals[7], totals[8], totals[9], totals[10], totals[11], totals[12], totals[13], totals[14])
```

```python
import functools

import jax
import jax.numpy as jnp
from jax import lax
from jax.experimental import pallas as pl
from jax.experimental.pallas import tpu as pltpu
from jax.sharding import PartitionSpec as P

GROUP = 8
EPS = 1e-05
BF = jnp.bfloat16
F32 = jnp.float32
AXES = ("dp", "mp")
SMALL = 96
CORE, PLANE, LINE = 1, 6, 24


def call(kernel, outs, *args, scratch=()):
    specs = [pl.BlockSpec(memory_space=pltpu.SMEM)]
    specs += [pl.BlockSpec(memory_space=pltpu.VMEM)] * (len(args) - 1)
    return pl.pallas_call(
        kernel,
        out_shape=[jax.ShapeDtypeStruct(s, t) for s, t in outs],
        in_specs=specs,
        out_specs=[pl.BlockSpec(memory_space=pltpu.VMEM)] * len(outs),
        scratch_shapes=list(scratch),
        compiler_params=pltpu.CompilerParams(vmem_limit_bytes=56 * 1024 * 1024),
    )(*args)


def at(start, size, align=128):
    return pl.ds(pl.multiple_of(start, align), size)


def dot(left, right):
    return jnp.dot(left, right, preferred_element_type=F32)


def dot_t(left, right):
    return lax.dot_general(left, right, (((1,), (1,)), ((), ())), preferred_element_type=F32)


def t_dot(left, right):
    return lax.dot_general(left, right, (((0,), (0,)), ((), ())), preferred_element_type=F32)


def row(ref):
    return ref[...].reshape(1, ref.shape[-1])


def prep_kernel(place, latent, cotangent, lat, hid, out, block, *pieces):
    top = 0
    for weight in (lat, hid, out):
        rows, columns = weight.shape
        for start in range(0, columns, 128):
            block[top : top + rows, :] = weight[:, start : start + 128].astype(BF)
            top += rows
    cut_features(place, (latent, cotangent), pieces)


def features_kernel(place, latent, cotangent, *pieces):
    cut_features(place, (latent, cotangent), pieces)


def cut_features(place, arrays, pieces):
    mine = place[0]
    rows = pieces[0].shape[1]
    for step, piece in enumerate(pieces):
        start = (mine ^ step) * rows
        for k, array in enumerate(arrays):
            piece[k] = array[at(start, rows), :]


def entry_kernel(place, ids, action, mask, table, act, task, bias, before, onehot, moves):
    mine = place[0]
    rows = before.shape[0]
    mine_ids = ids[pl.ds(mine, 1), :]
    tasks = table.shape[0]
    hot = (lax.broadcasted_iota(jnp.int32, (tasks, rows), 0) == mine_ids).astype(F32).astype(BF)
    onehot[...] = hot
    allowed = t_dot(hot, mask[...].astype(F32).astype(BF))
    moved = (action[at(mine * rows, rows), :].astype(F32) * allowed).astype(BF)
    moves[...] = moved
    vector = t_dot(hot, table[...].astype(BF)).astype(BF)
    before[...] = dot(vector, task[...].astype(BF)) + dot(moved, act[...].astype(BF)) + row(bias)


def norm(hidden, gain, shift):
    center = jnp.mean(hidden, -1, keepdims=True)
    spread = jnp.mean(hidden * hidden, -1, keepdims=True) - center * center
    scale = lax.rsqrt(spread + EPS)
    normal = (hidden - center) * scale
    return normal, scale, normal * gain + shift


def norm_mish(hidden, gain, shift):
    normal, scale, value = norm(hidden, gain, shift)
    grown = jnp.exp(jnp.minimum(value, 20.0))
    squares = grown * (grown + 2.0)
    inverse = 1.0 / (squares + 2.0)
    ratio = squares * inverse
    slope = ratio + 4.0 * value * (grown * (grown + 1.0)) * (inverse * inverse)
    return value * ratio, slope, normal, scale


def norm_mish_back(grad, slope, normal, scale, gain):
    through = grad * slope
    scaled = through * gain
    first = jnp.mean(scaled, -1, keepdims=True)
    second = jnp.mean(scaled * normal, -1, keepdims=True)
    low = (scale * (scaled - first - normal * second)).astype(BF)
    total = functools.partial(jnp.sum, axis=0, keepdims=True)
    return low, total(low.astype(F32)), total(through * normal), total(through)


def first_kernel(count, place, before, gain, shift, *rest):
    parts, pieces, (x, cot, lat, active, slope, normal, scale) = rest[:count], rest[count:-7], rest[-7:]
    mine = place[0]
    for step, piece in enumerate(pieces):
        start = at((mine ^ step) * 128, 128)
        x[:, start] = piece[0]
        cot[:, start] = piece[1]
    put_lat(place, parts, lat)
    hidden = dot(x[...], lat[...]) + before[...]
    value, slope[...], normal[...], scale[...] = norm_mish(hidden, row(gain), row(shift))
    active[...] = value.astype(BF)


def second_kernel(place, active_one, bias, gain, shift, *rest):
    parts, (hid, active, slope, normal, scale) = rest[:-5], rest[-5:]
    put_hid(place, parts, hid)
    hidden = dot(active_one[...], hid[...]) + row(bias)
    value, slope[...], normal[...], scale[...] = norm_mish(hidden, row(gain), row(shift))
    active[...] = value.astype(BF)


def group_sum(value, ones):
    high = value.astype(BF)
    low = (value - high.astype(F32)).astype(BF)
    return jnp.concatenate(
        [
            dot(high[:, k : k + 128], ones) + dot(low[:, k : k + 128], ones)
            for k in range(0, value.shape[1], 128)
        ],
        axis=1,
    )


def group_max(value):
    tops = []
    for k in range(0, value.shape[1], 128):
        top = value[:, k : k + 128]
        lane = lax.broadcasted_iota(jnp.int32, top.shape, 1)
        for step in (1, 2, 4):
            up, down = pltpu.roll(top, 128 - step, 1), pltpu.roll(top, step, 1)
            top = jnp.maximum(top, jnp.where((lane & step) == 0, up, down))
        tops.append(top)
    return jnp.concatenate(tops, axis=1)


def third_kernel(
    count, place, active_two, bias, gain, shift, cot, slope_two, normal_two, scale_two, gain_two, hid, active_one,
    slope_one, normal_one, scale_one, gain_one, lat, x, onehot, moves,
    *rest,
):
    parts, outs, (out, grad, small) = rest[:count], rest[count:-3], rest[-3:]
    (result, latent_pieces, grads) = outs[:4], outs[4:8], outs[8:]
    put_out(place, parts, out)
    hidden = dot(active_two[...], out[...]) + row(bias)
    normal, scale, value = norm(hidden, row(gain), row(shift))
    ones = (
        lax.broadcasted_iota(jnp.int32, (128, 128), 0) // GROUP
        == lax.broadcasted_iota(jnp.int32, (128, 128), 1) // GROUP
    ).astype(F32).astype(BF)
    grown = jnp.exp(value - group_max(value))
    share = grown / group_sum(grown, ones)
    cut_columns(place, share.astype(BF), result, grad)
    weighed = cot[...].astype(F32) * share
    through = weighed - share * group_sum(weighed, ones)
    total = functools.partial(jnp.sum, axis=0, keepdims=True)
    small[92:93, 0:512] = total(through * normal)
    small[92:93, 512:1024] = total(through)
    scaled = through * row(gain)
    first = jnp.mean(scaled, -1, keepdims=True)
    second = jnp.mean(scaled * normal, -1, keepdims=True)
    low = (scale * (scaled - first - normal * second)).astype(BF)
    small[93:94, 0:512] = total(low.astype(F32))
    small[93:94, 512:1024] = jnp.zeros((1, 512), F32)
    small[94:96, :] = jnp.zeros((2, 1024), F32)
    give_out(place, t_dot(active_two[...], low), grad, grads)

    back = dot_t(low, out[...])
    low, *sums = norm_mish_back(back, slope_two[...], normal_two[...], scale_two[...], row(gain_two))
    for k in range(3):
        small[89 + k : 90 + k, :] = sums[k]
    give_hid(place, t_dot(active_one[...], low), grad, grads)

    back = dot_t(low, hid[...])
    low, *sums = norm_mish_back(back, slope_one[...], normal_one[...], scale_one[...], row(gain_one))
    for k in range(3):
        small[86 + k : 87 + k, :] = sums[k]
    small[0:80, :] = dot(onehot[...], low)
    small[80:86, :] = t_dot(moves[...], low)
    give_lat(place, t_dot(x[...], low), grad, small, grads)
    cut_columns(place, dot_t(low, lat[...]).astype(BF), latent_pieces, grad)


def cut_columns(place, value, pieces, held):
    rows, columns = value.shape
    held[0:rows, 0:columns] = value
    for step, piece in enumerate(pieces):
        piece[...] = held[0:rows, at((place[0] ^ step) * 128, 128)]


def spots():
    for k in range(4):
        for z in range(4):
            yield k, z, 2 * z + k // 2, k % 2


def put_lat(place, parts, lat):
    if len(parts) == 1:
        lat[...] = parts[0][...]
        return
    core = place[0] & 1
    own, other = parts
    for k, z, i, x in spots():
        for part, c in ((own, core), (other, 1 - core)):
            for h in (0, 1):
                lat[64 * i : 64 * i + 64, at(256 * (2 * x + c) + 128 * h, 128)] = part[k, z, 64 * h : 64 * h + 64, :]


def put_hid(place, parts, hid):
    if len(parts) == 1:
        hid[...] = parts[0][...]
        return
    core = place[0] & 1
    own_a, other_a, own_b, other_b = parts
    for k, z, i, x in spots():
        for a, b, c in ((own_a, own_b, core), (other_a, other_b, 1 - core)):
            start = 256 * (2 * x + c)
            hid[at(start, 64), 128 * i : 128 * i + 128] = a[k, z, 128:192, :]
            hid[at(start + 64, 192, 64), 128 * i : 128 * i + 128] = b[k, z, :, :]


def put_out(place, parts, out):
    if len(parts) == 1:
        out[...] = parts[0][...]
        return
    core = place[0] & 1
    own, other = parts
    for k, z, i, x in spots():
        for part, c in ((own, core), (other, 1 - core)):
            out[128 * i : 128 * i + 128, at(128 * (2 * x + c), 128)] = part[k, z, :, :]


def give_out(place, value, grad, grads):
    if len(grads) == 4:
        grads[0][...] = value
        return
    core = place[0] & 1
    grad[0:1024, 0:512] = value.astype(BF)
    for k, z, i, x in spots():
        for part, c in ((grads[0], core), (grads[1], 1 - core)):
            part[k, z] = grad[128 * i : 128 * i + 128, at(128 * (2 * x + c), 128)]


def give_hid(place, value, grad, grads):
    if len(grads) == 4:
        grads[1][...] = value
        return
    core = place[0] & 1
    grad[0:1024, 0:1024] = value.astype(BF)
    for k, z, i, x in spots():
        for part, c in ((grads[2], core), (grads[3], 1 - core)):
            part[k, z] = grad[at(256 * (2 * x + c), 256), 128 * i : 128 * i + 128]


def give_lat(place, value, grad, small, grads):
    if len(grads) == 4:
        grads[2][...] = value
        grads[3][...] = small[...]
        return
    core = place[0] & 1
    grad[0:512, 0:1024] = value.astype(BF)
    for k, z, i, x in spots():
        for part, c in ((grads[4], core), (grads[5], 1 - core)):
            for h in (0, 1):
                part[k, 128 * z + 64 * h : 128 * z + 64 * h + 64, :] = grad[
                    64 * i : 64 * i + 64, at(256 * (2 * x + c) + 128 * h, 128)
                ]
    for k in range(4):
        for part, c in ((grads[4], core), (grads[5], 1 - core)):
            part[k, 512:608, :] = small[:, at((4 * c + k) * 128, 128)].astype(BF)


def join_kernel(place, out_own, out_in, hid_own, hid_in, lat_own, lat_in, joined):
    def add(a, b):
        return (a.astype(F32) + b.astype(F32)).astype(BF)

    for k in range(4):
        for z in range(4):
            top = 512 * z
            joined[k, top : top + 128, :] = add(lat_own[k, 128 * z : 128 * z + 128, :], lat_in[k, 128 * z : 128 * z + 128, :])
            joined[k, top + 128 : top + 384, :] = add(hid_own[k, z], hid_in[k, z])
            joined[k, top + 384 : top + 512, :] = add(out_own[k, z], out_in[k, z])
        joined[k, 2048:2144, :] = add(lat_own[k, 512:608, :], lat_in[k, 512:608, :])


def total_of(ref, rows):
    value = ref[0, rows, :].astype(F32)
    for k in range(1, ref.shape[0]):
        value = value + ref[k, rows, :].astype(F32)
    return value


def plane_kernel(place, parts, line):
    small = total_of(parts, slice(2048, 2144)).astype(BF)
    for z in range(4):
        line[z, 0:512, :] = total_of(parts, slice(512 * z, 512 * z + 512)).astype(BF)
        line[z, 512:608, :] = small


def line_kernel(place, parts, lat, hid, out, small):
    small[...] = total_of(parts, slice(512, 608)).astype(BF)
    lat[:, 0:128] = total_of(parts, slice(0, 64))
    lat[:, 128:256] = total_of(parts, slice(64, 128))
    hid[...] = total_of(parts, slice(128, 384))
    out[...] = total_of(parts, slice(384, 512))


def last_kernel(place, parts, table, task, *rest):
    pieces, outs, whole = rest[:8], rest[8:-1], rest[-1]
    if len(parts.shape) == 2:
        whole[...] = parts[...]
    else:
        for p in range(8):
            block = 4 * (p % 2) + p // 2
            whole[:, 128 * block : 128 * block + 128] = parts[p].astype(F32)
    result, latent, table_grad, act_grad, task_grad, *vectors = outs
    for out, kind in ((result, pieces[:4]), (latent, pieces[4:])):
        for step, piece in enumerate(kind):
            out[at((place[0] ^ step) * piece.shape[0], piece.shape[0]), :] = piece[...]
    by_task = whole[0:80, :].astype(BF)
    table_grad[...] = dot_t(by_task, task[...].astype(BF))
    task_grad[...] = t_dot(table[...].astype(BF), by_task)
    act_grad[...] = whole[80:86, :]
    for k in range(6):
        vectors[k][...] = whole[86 + k, :]
    vectors[6][...] = whole[93, 0:512]
    vectors[7][...] = whole[92, 0:512]
    vectors[8][...] = whole[92, 512:1024]


def groups_of(count, bits):
    kept = {}
    for n in range(count):
        kept.setdefault(n & ~bits, []).append(n)
    return list(kept.values())


def reduce_tree(place, weights, grads, swap, gather, exchange):
    out_own, out_send, hid_own, hid_send, lat_own, lat_send = grads
    hid_in, out_in, lat_in = swap(hid_send, CORE), swap(out_send, CORE), swap(lat_send, CORE)
    (joined,) = call(
        join_kernel, [((4, 2144, 128), BF)], place, out_own, out_in, hid_own, hid_in, lat_own, lat_in
    )
    (ready,) = call(plane_kernel, [((4, 608, 128), BF)], place, exchange(joined, PLANE))
    lat_grad, hid_grad, out_grad, small = call(
        line_kernel, [(w.shape, F32) for w in weights] + [((SMALL, 128), BF)], place, exchange(ready, LINE)
    )
    return lat_grad, hid_grad, out_grad, gather(small, CORE | PLANE)


def shards(
    mesh_shape, latent, action, task_ids, action_mask, cotangent, task_table, lat_weight, act_weight, task_weight,
    bias_one, gain_one, shift_one, hid_weight, bias_two, gain_two, shift_two, out_weight, bias_three, gain_three, shift_three,
):
    count = mesh_shape[0] * mesh_shape[1]
    mp = mesh_shape[1]
    rows = latent.shape[0] // mp
    place = lax.axis_index("mp").astype(jnp.int32).reshape(1)

    def swap(value, mask):
        return lax.ppermute(value, AXES, [(n, n ^ mask) for n in range(count)])

    def gather(value, bits):
        return lax.all_gather(value, AXES, axis_index_groups=groups_of(count, bits), axis=0)

    def exchange(value, bits):
        return lax.all_to_all(value, AXES, 0, 0, tiled=True, axis_index_groups=groups_of(count, bits))

    tree = mesh_shape == (8, 4)
    weights = (lat_weight, hid_weight, out_weight)
    cut = [((2, rows, 128), BF)] * mp
    if tree:
        block, *pieces = call(prep_kernel, [((512, 128), BF)] + cut, place, latent, cotangent, *weights)
    else:
        pieces = call(features_kernel, cut, place, latent, cotangent)
    pieces = [pieces[0]] + [swap(pieces[step], step) for step in range(1, mp)]
    before, onehot, moves = call(
        entry_kernel,
        [((rows, 1024), F32), ((80, rows), BF), ((rows, 6), BF)],
        place, task_ids.reshape(mp, rows), action, action_mask, task_table, act_weight, task_weight, bias_one,
    )
    if tree:
        lined = gather(block, LINE)
        chunks = []
        for start, stop in ((0, 192), (192, 384), (384, 512)):
            own = gather(lined[:, start:stop], PLANE)
            chunks.append((own, swap(own, CORE)))
        lat_parts, hid_parts, out_parts = chunks[0], chunks[0] + chunks[1], chunks[2]
    else:
        lat_parts, hid_parts, out_parts = [
            (lax.all_gather(lax.all_gather(w.astype(BF), down, axis=0, tiled=True), over, axis=1, tiled=True),)
            for w, (down, over) in zip(weights, (("dp", "mp"), ("mp", "dp"), ("dp", "mp")))
        ]
    wide = [((rows, 1024), BF), ((rows, 1024), F32), ((rows, 1024), F32), ((rows, 1), F32)]
    x, cot, lat, active_one, slope_one, normal_one, scale_one = call(
        functools.partial(first_kernel, len(lat_parts)),
        [((rows, 512), BF), ((rows, 512), BF), ((512, 1024), BF)] + wide,
        place, before, gain_one, shift_one, *lat_parts, *pieces,
    )
    hid, active_two, slope_two, normal_two, scale_two = call(
        second_kernel,
        [((1024, 1024), BF)] + wide,
        place, active_one, bias_two, gain_two, shift_two, *hid_parts,
    )
    if tree:
        sums = [((4, 4, 128, 128), BF)] * 2 + [((4, 4, 256, 128), BF)] * 2 + [((4, 608, 128), BF)] * 2
    else:
        sums = [((1024, 512), F32), ((1024, 1024), F32), ((512, 1024), F32), ((SMALL, 1024), F32)]
    outs = call(
        functools.partial(third_kernel, len(out_parts)),
        [((rows, 128), BF)] * 8 + sums,
        place, active_two, bias_three, gain_three, shift_three, cot,
        slope_two, normal_two, scale_two, gain_two, hid, active_one,
        slope_one, normal_one, scale_one, gain_one, lat, x, onehot, moves, *out_parts,
        scratch=[pltpu.VMEM((1024, 512), BF), pltpu.VMEM((1024, 1024), BF), pltpu.VMEM((SMALL, 1024), F32)],
    )
    sent = [outs[0]] + [swap(outs[k], k) for k in range(1, mp)]
    sent += [outs[4]] + [swap(outs[4 + k], k) for k in range(1, mp)]
    if tree:
        lat_grad, hid_grad, out_grad, parts = reduce_tree(place, weights, outs[8:], swap, gather, exchange)
    else:
        out_grad, hid_grad, lat_grad = [
            lax.psum_scatter(
                lax.psum_scatter(g, over, scatter_dimension=1, tiled=True), down, scatter_dimension=0, tiled=True
            )
            for g, (down, over) in zip(outs[8:11], (("dp", "mp"), ("mp", "dp"), ("dp", "mp")))
        ]
        parts = lax.psum(outs[11], AXES)
    final = call(
        last_kernel,
        [(latent.shape, BF)] * 2
        + [(task_table.shape, F32), (act_weight.shape, F32), (task_weight.shape, F32)]
        + [((1024,), F32)] * 6
        + [((512,), F32)] * 3,
        place, parts, task_table, task_weight, *sent,
        scratch=[pltpu.VMEM((SMALL, 1024), F32)],
    )
    result, latent_grad, table_grad, act_grad, task_grad, *vectors = final
    return (
        result, latent_grad, table_grad, lat_grad, act_grad, task_grad, *vectors[0:3], hid_grad, *vectors[3:6],
        out_grad, *vectors[6:9],
    )


def solution(mesh):
    both = P("dp", "mp")
    turned = P("mp", "dp")
    whole = P()
    return jax.shard_map(
        functools.partial(shards, (mesh.shape["dp"], mesh.shape["mp"])),
        mesh=mesh,
        in_specs=(
            both, P("dp", None), P("dp"), whole, both, whole, both, whole, whole, whole, whole, whole,
            turned, whole, whole, whole, both, whole, whole, whole,
        ),
        out_specs=(
            both, both, whole, both, whole, whole, whole, whole, whole, turned, whole, whole, whole, both,
            whole, whole, whole,
        ),
        check_vma=False,
    )
```

```python
import functools
import math

import jax
import jax.numpy as jnp
from jax import lax
from jax.experimental import pallas as pl
from jax.experimental.pallas import tpu as pltpu
from jax.sharding import PartitionSpec as P

GROUP = 8
EPS = 1e-05
BF = jnp.bfloat16
F32 = jnp.float32
AXES = ("dp", "mp")
SMALL = 96


def call(kernel, outs, *args, scratch=(), far=False):
    specs = [pl.BlockSpec(memory_space=pltpu.SMEM)]
    specs += [pl.BlockSpec(memory_space=pltpu.HBM if far else pltpu.VMEM)] * (len(args) - 1)
    if far:
        args = (args[0], *(pltpu.with_memory_space_constraint(a, pltpu.HBM) for a in args[1:]))
    held = [(a.shape, a.dtype) for a in args] + [*outs]
    held += [(s.shape, s.dtype) for s in scratch if s.memory_space == pltpu.VMEM]
    return pl.pallas_call(
        kernel,
        out_shape=[jax.ShapeDtypeStruct(s, t) for s, t in outs],
        in_specs=specs,
        out_specs=[pl.BlockSpec(memory_space=pltpu.VMEM)] * len(outs),
        scratch_shapes=list(scratch),
        compiler_params=pltpu.CompilerParams(
            vmem_limit_bytes=sum(math.prod(s) * jnp.dtype(t).itemsize for s, t in held) + (4 << 20)
        ),
        cost_estimate=pl.CostEstimate(flops=1, bytes_accessed=1, transcendentals=0),
    )(*args)


def at(start, size, align=128):
    return pl.ds(pl.multiple_of(start, align), size)


def dot(left, right):
    return jnp.dot(left, right, preferred_element_type=F32)


def dot_t(left, right):
    return lax.dot_general(left, right, (((1,), (1,)), ((), ())), preferred_element_type=F32)


def t_dot(left, right):
    return lax.dot_general(left, right, (((0,), (0,)), ((), ())), preferred_element_type=F32)


def fetch(pairs, sems):
    copies = [pltpu.make_async_copy(source, target, sems.at[k]) for k, (source, target) in enumerate(pairs)]
    for copy in copies:
        copy.start()
    for copy in copies:
        copy.wait()


def prep_kernel(count, place, *rest):
    sources, rest = rest[:count], rest[count:]
    pieces, blocks, held, sems = rest[:4], rest[4 : -count - 1], rest[-count - 1 : -1], rest[-1]
    fetch(tuple(zip(sources, held)), sems)
    if blocks:
        (first, second), (lat, hid, out) = blocks, held[2:]
        first[0:64, :] = lat[:, 0:128].astype(BF)
        first[64:128, :] = lat[:, 128:256].astype(BF)
        first[128:256, :] = hid[0:128, :].astype(BF)
        second[0:128, :] = hid[128:256, :].astype(BF)
        second[128:256, :] = out[...].astype(BF)
    rows = pieces[0].shape[1]
    for step, piece in enumerate(pieces):
        for k, features in enumerate(held[:2]):
            piece[k] = features[at((place[0] ^ step) * rows, rows), :]


def entry_kernel(count, place, *rest):
    sources, (before, onehot, moves, vectors), held, sems = rest[:count], rest[count : count + 4], rest[count + 4 : -1], rest[-1]
    fetch(tuple(zip(sources, held)), sems)
    ids, action, mask, table, act, task, *rows_held = held
    rows = before.shape[0]
    mine = place[0]
    hot = lax.broadcasted_iota(jnp.int32, (table.shape[0], rows), 0) == ids[:, at(mine * rows, rows)]
    hot = hot.astype(F32).astype(BF)
    onehot[...] = hot
    allowed = dot(mask[...].astype(F32).astype(BF), hot)
    moved = (action[:, at(mine * rows, rows)].astype(F32) * allowed).astype(BF)
    moves[...] = moved
    vector = t_dot(hot, table[...].astype(BF)).astype(BF)
    for k, held_row in enumerate(rows_held):
        vectors[k : k + 1, 0 : held_row.shape[1]] = held_row[...]
    before[...] = dot(vector, task[...].astype(BF)) + t_dot(moved, act[...].astype(BF)) + vectors[0:1, :]


def norm(hidden, gain, shift):
    center = jnp.mean(hidden, -1, keepdims=True)
    spread = jnp.mean(hidden * hidden, -1, keepdims=True) - center * center
    scale = lax.rsqrt(spread + EPS)
    normal = (hidden - center) * scale
    return normal, scale, normal * gain + shift


def norm_mish(hidden, gain, shift):
    normal, scale, value = norm(hidden, gain, shift)
    grown = jnp.exp(jnp.minimum(value, 20.0))
    squares = grown * (grown + 2.0)
    inverse = 1.0 / (squares + 2.0)
    ratio = squares * inverse
    slope = ratio + 4.0 * value * (grown * (grown + 1.0)) * (inverse * inverse)
    return value * ratio, slope, normal, scale


def norm_mish_back(grad, slope, normal, scale, gain):
    through = grad * slope
    scaled = through * gain
    first = jnp.mean(scaled, -1, keepdims=True)
    second = jnp.mean(scaled * normal, -1, keepdims=True)
    low = (scale * (scaled - first - normal * second)).astype(BF)
    total = functools.partial(jnp.sum, axis=0, keepdims=True)
    return low, total(low.astype(F32)), total(through * normal), total(through)


def first_kernel(count, place, before, vectors, *rest):
    parts, pieces, (x, cot, lat, active, slope, normal, scale) = rest[:count], rest[count:-7], rest[-7:]
    mine = place[0]
    for step, piece in enumerate(pieces):
        start = at((mine ^ step) * 128, 128)
        x[:, start] = piece[0]
        cot[:, start] = piece[1]
    put_lat(place, parts, lat)
    hidden = dot(x[...], lat[...]) + before[...]
    value, slope[...], normal[...], scale[...] = norm_mish(hidden, vectors[1:2, :], vectors[2:3, :])
    active[...] = value.astype(BF)


def second_kernel(place, active_one, vectors, *rest):
    parts, (hid, active, slope, normal, scale) = rest[:-5], rest[-5:]
    put_hid(place, parts, hid)
    hidden = dot(active_one[...], hid[...]) + vectors[3:4, :]
    value, slope[...], normal[...], scale[...] = norm_mish(hidden, vectors[4:5, :], vectors[5:6, :])
    active[...] = value.astype(BF)


def group_sum(value, ones):
    high = value.astype(BF)
    low = (value - high.astype(F32)).astype(BF)
    return jnp.concatenate(
        [
            dot(high[:, k : k + 128], ones) + dot(low[:, k : k + 128], ones)
            for k in range(0, value.shape[1], 128)
        ],
        axis=1,
    )


def group_max(value):
    tops = []
    for k in range(0, value.shape[1], 128):
        top = value[:, k : k + 128]
        lane = lax.broadcasted_iota(jnp.int32, top.shape, 1)
        for step in (1, 2, 4):
            up, down = pltpu.roll(top, 128 - step, 1), pltpu.roll(top, step, 1)
            top = jnp.maximum(top, jnp.where((lane & step) == 0, up, down))
        tops.append(top)
    return jnp.concatenate(tops, axis=1)


def third_kernel(
    count, place, active_two, vectors, cot, slope_two, normal_two, scale_two, hid, active_one, *rest,
):
    parts, outs, (out, grad) = rest[:count], rest[count:-2], rest[-2:]
    (result, low_two, small), grads = outs[:3], outs[3:]
    put_out(place, parts, out)
    hidden = dot(active_two[...], out[...]) + vectors[6:7, 0:512]
    gain = vectors[7:8, 0:512]
    normal, scale, value = norm(hidden, gain, vectors[8:9, 0:512])
    ones = (
        lax.broadcasted_iota(jnp.int32, (128, 128), 0) // GROUP
        == lax.broadcasted_iota(jnp.int32, (128, 128), 1) // GROUP
    ).astype(F32).astype(BF)
    grown = jnp.exp(value - group_max(value))
    share = grown / group_sum(grown, ones)
    result[...] = share.astype(BF)
    weighed = cot[...].astype(F32) * share
    through = weighed - share * group_sum(weighed, ones)
    total = functools.partial(jnp.sum, axis=0, keepdims=True)
    small[3:4, 0:512] = total(through * normal)
    small[3:4, 512:1024] = total(through)
    scaled = through * gain
    first = jnp.mean(scaled, -1, keepdims=True)
    second = jnp.mean(scaled * normal, -1, keepdims=True)
    low = (scale * (scaled - first - normal * second)).astype(BF)
    small[4:5, 0:512] = total(low.astype(F32))
    small[4:5, 512:1024] = jnp.zeros((1, 512), F32)
    small[5:8, :] = jnp.zeros((3, 1024), F32)
    give_out(place, t_dot(active_two[...], low), grad, grads)

    back = dot_t(low, out[...])
    low, *sums = norm_mish_back(back, slope_two[...], normal_two[...], scale_two[...], vectors[4:5, :])
    low_two[...] = low
    for k in range(3):
        small[k : k + 1, :] = sums[k]
    give_hid(place, t_dot(active_one[...], low), grad, grads)


def fourth_kernel(
    count, place, share, low_two, small_two, vectors, hid, slope_one, normal_one, scale_one, lat, x, onehot, moves, *rest,
):
    halves, pieces, grads, (grad, small) = rest[:count], rest[count : count + 4], rest[count + 4 : -2], rest[-2:]
    back = dot_t(low_two[...], hid[...])
    low, *sums = norm_mish_back(back, slope_one[...], normal_one[...], scale_one[...], vectors[1:2, :])
    for k in range(3):
        small[86 + k : 87 + k, :] = sums[k]
    small[89:94, :] = small_two[0:5, :]
    small[94:96, :] = jnp.zeros((2, 1024), F32)
    small[0:80, :] = dot(onehot[...], low)
    small[80:86, :] = dot(moves[...], low)
    give_lat(place, t_dot(x[...], low), grad, small, halves, grads)
    rows = share.shape[0]
    grad[0:rows, 0:512] = dot_t(low, lat[...]).astype(BF)
    for step, piece in enumerate(pieces):
        start = at((place[0] ^ step) * 128, 128)
        piece[0] = share[:, start]
        piece[1] = grad[0:rows, start]


def spots(place, c):
    _, x, y, z, core = [place[n] for n in range(5)]
    for k in range(4):
        for far in range(4):
            yield k, far, 2 * (z ^ far) + (y ^ (k >> 1)), 2 * (x ^ (k & 1)) + (core ^ c)


def part_of(parts, c, k, far, half):
    part = parts[4 * c + k]
    return part.at[far] if len(part.shape) == 3 else part.at[half, far]


def put_lat(place, parts, lat):
    if len(parts) == 1:
        lat[...] = parts[0][...]
        return
    for c in range(2):
        for k, far, i, j in spots(place, c):
            block = part_of(parts, c, k, far, 0)
            for h in range(2):
                lat[at(64 * i, 64, 64), at(256 * j + 128 * h, 128)] = block[64 * h : 64 * h + 64, :]


def put_hid(place, parts, hid):
    if len(parts) == 1:
        hid[...] = parts[0][...]
        return
    for c in range(2):
        for k, far, i, j in spots(place, c):
            hid[at(256 * j, 128), at(128 * i, 128)] = part_of(parts[:8], c, k, far, 1)[...]
            hid[at(256 * j + 128, 128), at(128 * i, 128)] = part_of(parts[8:], c, k, far, 0)[...]


def put_out(place, parts, out):
    if len(parts) == 1:
        out[...] = parts[0][...]
        return
    for c in range(2):
        for k, far, i, j in spots(place, c):
            out[at(128 * i, 128), at(128 * j, 128)] = part_of(parts, c, k, far, 1)[...]


def give_out(place, value, grad, grads):
    if len(grads) == 2:
        grads[0][...] = value
        return
    grad[0:1024, 0:512] = value.astype(BF)
    for c in range(2):
        for k, far, i, j in spots(place, c):
            grads[c][k, 256 * far + 128 : 256 * far + 256, :] = grad[at(128 * i, 128), at(128 * j, 128)]


def give_hid(place, value, grad, grads):
    if len(grads) == 2:
        grads[1][...] = value
        return
    grad[0:1024, 0:1024] = value.astype(BF)
    for c in range(2):
        for k, far, i, j in spots(place, c):
            grads[2 + c][k, far] = grad[at(256 * j, 128), at(128 * i, 128)]
            grads[c][k, 256 * far : 256 * far + 128, :] = grad[at(256 * j + 128, 128), at(128 * i, 128)]


def give_lat(place, value, grad, small, halves, grads):
    if not halves:
        grads[0][...] = value
        grads[1][...] = small[...]
        return
    grad[0:512, 0:1024] = value.astype(BF)
    for c in range(2):
        for k, far, i, j in spots(place, c):
            top = 256 * far
            for h in range(2):
                grads[c][k, top + 64 * h : top + 64 * h + 64, :] = grad[at(64 * i, 64, 64), at(256 * j + 128 * h, 128)]
            grads[c][k, top + 128 : top + 256, :] = halves[c][k, far]
            if far == 0:
                grads[c][k, 1024:1120, :] = small[:, at(small_column(place, k, c), 128)].astype(BF)


def small_column(place, k, c):
    _, x, y, _, core = [place[n] for n in range(5)]
    return 128 * (4 * (core ^ c) + 2 * (y ^ (k >> 1)) + (x ^ (k & 1)))


def plus(*values):
    return functools.reduce(lambda a, b: a + b, (v.astype(F32) for v in values))


def chunk_kernel(place, *rest):
    blocks, chunks = rest[:8], rest[8:]
    for n, block in enumerate(blocks):
        chunks[n // 4][0, n % 4] = block[0:128, :]
        chunks[n // 4][1, n % 4] = block[128:256, :]


def join_kernel(place, kept, came, own, by_x, by_y, cross_y, cross_x):
    for k, out in enumerate((own, by_x, by_y)):
        out[...] = kept[k] + came[k]
    half = cross_x.shape[0]
    cross_y[...] = kept[3, :half, :] + came[3, :half, :]
    cross_x[...] = kept[3, half:, :] + came[3, half:, :]


def cross_kernel(place, by_x, by_y, from_y, from_x, to_x, to_y):
    half = from_x.shape[0]
    to_x[:half, :] = by_x[:half, :] + from_y[...]
    to_x[half:, :] = by_x[half:, :]
    to_y[:half, :] = by_y[:half, :]
    to_y[half:, :] = by_y[half:, :] + from_x[...]


def plane_kernel(place, own, from_x, from_y, kept, near, middle, far):
    for out, step in ((kept, 0), (near, 1), (middle, 2), (far, 3)):
        rows = slice(256 * step, 256 * step + 256)
        out[0:256, :] = plus(own[rows, :], from_x[rows, :], from_y[rows, :]).astype(out.dtype)
    if far.shape[0] > 256:
        far[256:, :] = plus(own[1024:, :], from_x[1024:, :], from_y[1024:, :]).astype(BF)


def line_kernel(place, middle, far, came, to_middle):
    to_middle[0:256, :] = middle[...] + came[0:256, :]
    if far.shape[0] > 256:
        to_middle[256:, :] = plus(far[256:, :], came[256:, :]).astype(BF)


def small_kernel(place, to_middle, came, small):
    small[...] = plus(to_middle[256:, :], came[256:, :]).astype(BF)


def finish_kernel(place, *rest):
    (kept_a, near_a, middle_a, kept_b, near_b, middle_b), pieces, outs = rest[:6], rest[6:-5], rest[-5:]
    lat, hid, out, *features = outs

    def total(rows, chunk):
        return plus(*(ref[rows, :] for ref in chunk))

    first, second = (kept_a, near_a, middle_a), (kept_b, near_b, middle_b)
    lat[:, 0:128] = total(slice(0, 64), first)
    lat[:, 128:256] = total(slice(64, 128), first)
    hid[0:128, :] = total(slice(128, 256), first)
    hid[128:256, :] = total(slice(0, 128), second)
    out[...] = total(slice(128, 256), second)
    put_features(place, pieces, features)


def put_features(place, pieces, outs):
    for step, piece in enumerate(pieces):
        rows = piece.shape[1]
        for k, out in enumerate(outs):
            out[at((place[0] ^ step) * rows, rows), :] = piece[k]


def rows_kernel(place, *rest):
    put_features(place, rest[:-2], rest[-2:])


def last_kernel(count, place, *rest):
    parts, (table, task), outs, whole = rest[:count], rest[count : count + 2], rest[count + 2 : -1], rest[-1]
    if count == 1:
        whole[...] = parts[0][...]
    for n, part in enumerate(parts if count > 1 else ()):
        whole[:, at(small_column(place, n & 3, n >> 2), 128)] = part[...].astype(F32)
    table_grad, act_grad, task_grad, *vectors = outs
    by_task = whole[0:80, :].astype(BF)
    table_grad[...] = dot_t(by_task, task[...].astype(BF))
    task_grad[...] = t_dot(table[...].astype(BF), by_task)
    act_grad[...] = whole[80:86, :]
    for k in range(6):
        vectors[k][...] = whole[86 + k, :]
    vectors[6][...] = whole[93, 0:512]
    vectors[7][...] = whole[92, 0:512]
    vectors[8][...] = whole[92, 512:1024]


CORE, X, Y, NEAR, MIDDLE = 1, 2, 4, 8, 16


def gather_line(block, swap):
    middle, near = swap(block, MIDDLE), swap(block, NEAR)
    return block, near, middle, swap(middle, NEAR)


def gather_plane(own, swap):
    from_x, from_y = swap(own, X), swap(own, Y)
    return [own, from_x, from_y, swap(from_x[0], Y), swap(from_y[1], X)]


def sides(parts, half):
    own, other = parts
    return [p for side in (own, other) for p in (*side[:3], side[3 + half])]


def reduce_plane(place, kept, sent, swap):
    rows = kept.shape[1]
    came = swap(sent, CORE)
    full, half = ((rows, 128), BF), ((rows // 2, 128), BF)
    own, by_x, by_y, cross_y, cross_x = call(join_kernel, [full] * 3 + [half] * 2, place, kept, came)
    to_x, to_y = call(cross_kernel, [full] * 2, place, by_x, by_y, swap(cross_y, Y), swap(cross_x, X))
    return own, swap(to_x, X), swap(to_y, Y)


def reduce_line(place, own, from_x, from_y, swap):
    block = ((256, 128), BF)
    more = ((own.shape[0] - 768, 128), BF)
    kept, near, middle, far = call(
        plane_kernel, [((256, 128), F32), block, block, more], place, own, from_x, from_y
    )
    (to_middle,) = call(line_kernel, [more], place, middle, far, swap(far, NEAR))
    return kept, swap(near, NEAR), swap(to_middle, MIDDLE), to_middle


def shards(
    mesh_shape, latent, action, task_ids, action_mask, cotangent, task_table, lat_weight, act_weight, task_weight,
    bias_one, gain_one, shift_one, hid_weight, bias_two, gain_two, shift_two, out_weight, bias_three, gain_three, shift_three,
):
    count = mesh_shape[0] * mesh_shape[1]
    mp = mesh_shape[1]
    rows = latent.shape[0] // mp
    column, line = lax.axis_index("mp"), lax.axis_index("dp")
    place = jnp.stack([column, column >> 1, line & 1, line >> 1, column & 1]).astype(jnp.int32)

    def swap(value, mask):
        return lax.ppermute(value, AXES, [(n, n ^ mask) for n in range(count)])

    tree = mesh_shape == (8, 4)
    weights = (lat_weight, hid_weight, out_weight)
    small_args = (
        task_ids.reshape(1, -1), action.T, action_mask.T, task_table, act_weight, task_weight,
        *(v.reshape(1, -1) for v in (
            bias_one, gain_one, shift_one, bias_two, gain_two, shift_two, bias_three, gain_three, shift_three,
        )),
    )
    sources = (latent, cotangent, *weights) if tree else (latent, cotangent)
    outs = call(
        functools.partial(prep_kernel, len(sources)),
        [((2, rows, 128), BF)] * mp + [((256, 128), BF)] * (2 if tree else 0),
        place, *sources,
        scratch=[pltpu.VMEM(v.shape, v.dtype) for v in sources] + [pltpu.SemaphoreType.DMA((len(sources),))],
        far=True,
    )
    pieces, blocks = outs[:mp], outs[mp:]
    pieces = [pieces[0]] + [swap(pieces[step], step) for step in range(1, mp)]
    before, onehot, moves, vectors = call(
        functools.partial(entry_kernel, len(small_args)),
        [((rows, 1024), F32), ((80, rows), BF), ((6, rows), BF), ((16, 1024), F32)],
        place, *small_args,
        scratch=[pltpu.VMEM(v.shape, v.dtype) for v in small_args] + [pltpu.SemaphoreType.DMA((len(small_args),))],
        far=True,
    )
    if tree:
        lines = [gather_line(block, swap) for block in blocks]
        lines, pieces, before = lax.optimization_barrier((lines, pieces, before))
        chunks = call(chunk_kernel, [((2, 4, 128, 128), BF)] * 2, place, *lines[0], *lines[1])
        chunks = [gather_plane(chunk, swap) for chunk in chunks]
        chunks = [(side, [swap(part, CORE) for part in side]) for side in chunks]
        lat_parts = sides(chunks[0], 0)
        hid_parts = sides(chunks[0], 1) + sides(chunks[1], 0)
        out_parts = sides(chunks[1], 1)
    else:
        lat_parts, hid_parts, out_parts = [
            (lax.all_gather(lax.all_gather(w.astype(BF), down, axis=0, tiled=True), over, axis=1, tiled=True),)
            for w, (down, over) in zip(weights, (("dp", "mp"), ("mp", "dp"), ("dp", "mp")))
        ]
    wide = [((rows, 1024), BF), ((rows, 1024), F32), ((rows, 1024), F32), ((rows, 1), F32)]
    x, cot, lat, active_one, slope_one, normal_one, scale_one = call(
        functools.partial(first_kernel, len(lat_parts)),
        [((rows, 512), BF), ((rows, 512), BF), ((512, 1024), BF)] + wide,
        place, before, vectors, *lat_parts, *pieces,
    )
    hid, active_two, slope_two, normal_two, scale_two = call(
        second_kernel, [((1024, 1024), BF)] + wide, place, active_one, vectors, *hid_parts
    )
    if tree:
        sums = [((4, 1024, 128), BF)] * 2 + [((4, 4, 128, 128), BF)] * 2
    else:
        sums = [((1024, 512), F32), ((1024, 1024), F32)]
    outs = call(
        functools.partial(third_kernel, len(out_parts)),
        [((rows, 512), BF), ((rows, 1024), BF), ((8, 1024), F32)] + sums,
        place, active_two, vectors, cot, slope_two, normal_two, scale_two, hid, active_one, *out_parts,
        scratch=[pltpu.VMEM((1024, 512), BF), pltpu.VMEM((1024, 1024), BF)],
    )
    share, low_two, small_two, give_a, give_b, *halves = outs
    *finals, lat_a, lat_b = call(
        functools.partial(fourth_kernel, len(halves)),
        [((2, rows, 128), BF)] * mp
        + ([((4, 1120, 128), BF)] * 2 if tree else [((512, 1024), F32), ((SMALL, 1024), F32)]),
        place, share, low_two, small_two, vectors, hid, slope_one, normal_one, scale_one, lat, x, onehot, moves, *halves,
        scratch=[pltpu.VMEM((512, 1024), BF), pltpu.VMEM((SMALL, 1024), F32)],
    )
    finals = [swap(piece, step) if step else piece for step, piece in enumerate(finals)]
    features = [(latent.shape, BF)] * 2
    if tree:
        first = reduce_plane(place, lat_a, lat_b, swap)
        second = reduce_plane(place, give_a, give_b, swap)
        *first, to_middle = reduce_line(place, *first, swap)
        *second, _ = reduce_line(place, *second, swap)
        (small,) = call(small_kernel, [((SMALL, 128), BF)], place, to_middle, first[2])
        parts = [small, swap(small, X), swap(small, Y), swap(small, X | Y)]
        parts += [swap(part, CORE) for part in parts]
        lat_grad, hid_grad, out_grad, result, latent_grad = call(
            finish_kernel, [(w.shape, F32) for w in weights] + features, place, *first, *second, *finals
        )
    else:
        out_grad, hid_grad, lat_grad = [
            lax.psum_scatter(
                lax.psum_scatter(g, over, scatter_dimension=1, tiled=True), down, scatter_dimension=0, tiled=True
            )
            for g, (down, over) in zip((give_a, give_b, lat_a), (("dp", "mp"), ("mp", "dp"), ("dp", "mp")))
        ]
        parts = [lax.psum(lat_b, AXES)]
        result, latent_grad = call(rows_kernel, features, place, *finals)
    table_grad, act_grad, task_grad, *vector_grads = call(
        functools.partial(last_kernel, len(parts)),
        [(task_table.shape, F32), (act_weight.shape, F32), (task_weight.shape, F32)]
        + [((1024,), F32)] * 6
        + [((512,), F32)] * 3,
        place, *parts, task_table, task_weight,
        scratch=[pltpu.VMEM((SMALL, 1024), F32)],
    )
    return (
        result, latent_grad, table_grad, lat_grad, act_grad, task_grad, *vector_grads[0:3], hid_grad, *vector_grads[3:6],
        out_grad, *vector_grads[6:9],
    )


def solution(mesh):
    both = P("dp", "mp")
    turned = P("mp", "dp")
    whole = P()
    return jax.shard_map(
        functools.partial(shards, (mesh.shape["dp"], mesh.shape["mp"])),
        mesh=mesh,
        in_specs=(
            both, P("dp", None), P("dp"), whole, both, whole, both, whole, whole, whole, whole, whole,
            turned, whole, whole, whole, both, whole, whole, whole,
        ),
        out_specs=(
            both, both, whole, both, whole, whole, whole, whole, whole, turned, whole, whole, whole, both,
            whole, whole, whole,
        ),
        check_vma=False,
    )
```

```python
import functools
import math

import jax
import jax.numpy as jnp
from jax import lax
from jax.experimental import pallas as pl
from jax.experimental.pallas import tpu as pltpu
from jax.sharding import PartitionSpec as P

GROUP = 8
EPS = 1e-05
BF = jnp.bfloat16
F32 = jnp.float32
AXES = ("dp", "mp")
SMALL = 96

SCALE = 4e9
COST = {
    "prep_kernel": 1.7, "entry_kernel": 2.2, "first_kernel": 1.5, "second_kernel": 2.0, "third_kernel": 2.7,
    "fourth_kernel": 2.1, "fifth_kernel": 1.3, "sixth_kernel": 0.1, "join_kernel": 0.5, "chunk_kernel": 0.5,
}


def call(kernel, outs, *args, scratch=(), far=False, cost=None):
    cost = COST.get(getattr(kernel, "func", kernel).__name__, 0) if cost is None else cost
    if far:
        args = [pltpu.with_memory_space_constraint(a, pltpu.HBM) for a in args]
    held = [(a.shape, a.dtype) for a in args] + [*outs]
    held += [(s.shape, s.dtype) for s in scratch if s.memory_space == pltpu.VMEM]
    return pl.pallas_call(
        kernel,
        out_shape=[jax.ShapeDtypeStruct(s, t) for s, t in outs],
        in_specs=[pl.BlockSpec(memory_space=pltpu.HBM if far else pltpu.VMEM)] * len(args),
        out_specs=[pl.BlockSpec(memory_space=pltpu.VMEM)] * len(outs),
        scratch_shapes=list(scratch),
        compiler_params=pltpu.CompilerParams(
            vmem_limit_bytes=sum(math.prod(s) * jnp.dtype(t).itemsize for s, t in held) + (4 << 20)
        ),
        cost_estimate=pl.CostEstimate(flops=int(cost * SCALE), bytes_accessed=0, transcendentals=0),
    )(*args)


def place_of():
    column, line = lax.axis_index("mp"), lax.axis_index("dp")
    return column >> 1, line & 1, line >> 1, column & 1


def at(start, size, align=128):
    return pl.ds(pl.multiple_of(start, align), size)


def dot(left, right):
    return jnp.dot(left, right, preferred_element_type=F32)


def dot_t(left, right):
    return lax.dot_general(left, right, (((1,), (1,)), ((), ())), preferred_element_type=F32)


def t_dot(left, right):
    return lax.dot_general(left, right, (((0,), (0,)), ((), ())), preferred_element_type=F32)


def fetch(pairs, sems):
    copies = [pltpu.make_async_copy(source, target, sems.at[k]) for k, (source, target) in enumerate(pairs)]
    for copy in copies:
        copy.start()
    for copy in copies:
        copy.wait()


def prep_kernel(count, *rest):
    sources, rest = rest[:count], rest[count:]
    own, beside, across, *blocks = rest[: -count - 1]
    held, sems = rest[-count - 1 : -1], rest[-1]
    fetch(tuple(zip(sources, held)), sems)
    mine, rows = lax.axis_index("mp"), own.shape[1]
    for step, piece in enumerate((own, beside.at[0], across, beside.at[1])):
        for k, features in enumerate(held[:2]):
            piece[k] = features[at((mine ^ step) * rows, rows), :]
    if blocks:
        (block,), (lat, hid, out) = blocks, held[2:]
        block[0:64, :] = lat[:, 0:128].astype(BF)
        block[64:128, :] = lat[:, 128:256].astype(BF)
        block[128:384, :] = hid[...].astype(BF)
        block[384:512, :] = out[...].astype(BF)


def entry_kernel(count, *rest):
    sources, (before, onehot, moves, vectors), held, sems = rest[:count], rest[count : count + 4], rest[count + 4 : -1], rest[-1]
    fetch(tuple(zip(sources, held)), sems)
    ids, action, mask, table, act, task, *rows_held = held
    rows = before.shape[0]
    mine = lax.axis_index("mp")
    hot = lax.broadcasted_iota(jnp.int32, (table.shape[0], rows), 0) == ids[:, at(mine * rows, rows)]
    hot = hot.astype(F32).astype(BF)
    onehot[...] = hot
    allowed = dot(mask[...].astype(F32).astype(BF), hot)
    moved = (action[:, at(mine * rows, rows)].astype(F32) * allowed).astype(BF)
    moves[...] = moved
    vector = t_dot(hot, table[...].astype(BF)).astype(BF)
    for k, held_row in enumerate(rows_held):
        vectors[k : k + 1, 0 : held_row.shape[1]] = held_row[...]
    before[...] = dot(vector, task[...].astype(BF)) + t_dot(moved, act[...].astype(BF)) + vectors[0:1, :]


def norm(hidden, gain, shift):
    center = jnp.mean(hidden, -1, keepdims=True)
    spread = jnp.mean(hidden * hidden, -1, keepdims=True) - center * center
    scale = lax.rsqrt(spread + EPS)
    normal = (hidden - center) * scale
    return normal, scale, normal * gain + shift


def norm_mish(hidden, gain, shift):
    normal, scale, value = norm(hidden, gain, shift)
    grown = jnp.exp(jnp.minimum(value, 20.0))
    squares = grown * (grown + 2.0)
    inverse = 1.0 / (squares + 2.0)
    ratio = squares * inverse
    slope = ratio + 4.0 * value * (grown * (grown + 1.0)) * (inverse * inverse)
    return value * ratio, slope, normal, scale


def norm_mish_back(grad, slope, normal, scale, gain):
    through = grad * slope
    scaled = through * gain
    first = jnp.mean(scaled, -1, keepdims=True)
    second = jnp.mean(scaled * normal, -1, keepdims=True)
    low = (scale * (scaled - first - normal * second)).astype(BF)
    total = functools.partial(jnp.sum, axis=0, keepdims=True)
    return low, total(low.astype(F32)), total(through * normal), total(through)


def first_kernel(count, before, vectors, *rest):
    parts, pieces, (x, cot, lat, active, slope, normal, scale) = rest[:count], rest[count:-7], rest[-7:]
    mine = lax.axis_index("mp")
    pieces = (pieces[0], pieces[1].at[0], *(pieces[2].at[n : n + 2] for n in range(pieces[2].shape[0] - 4, pieces[2].shape[0], 2)))
    for step, piece in enumerate(pieces):
        start = at((mine ^ step) * 128, 128)
        x[:, start] = piece[0]
        cot[:, start] = piece[1]
    put_lat(parts, lat)
    hidden = dot(x[...], lat[...]) + before[...]
    value, slope[...], normal[...], scale[...] = norm_mish(hidden, vectors[1:2, :], vectors[2:3, :])
    active[...] = value.astype(BF)


def second_kernel(active_one, vectors, *rest):
    parts, (hid, active, slope, normal, scale) = rest[:-5], rest[-5:]
    put_hid(parts, hid)
    hidden = dot(active_one[...], hid[...]) + vectors[3:4, :]
    value, slope[...], normal[...], scale[...] = norm_mish(hidden, vectors[4:5, :], vectors[5:6, :])
    active[...] = value.astype(BF)


def group_sum(value, ones):
    high = value.astype(BF)
    low = (value - high.astype(F32)).astype(BF)
    return jnp.concatenate(
        [
            dot(high[:, k : k + 128], ones) + dot(low[:, k : k + 128], ones)
            for k in range(0, value.shape[1], 128)
        ],
        axis=1,
    )


def group_max(value):
    tops = []
    for k in range(0, value.shape[1], 128):
        top = value[:, k : k + 128]
        lane = lax.broadcasted_iota(jnp.int32, top.shape, 1)
        for step in (1, 2, 4):
            up, down = pltpu.roll(top, 128 - step, 1), pltpu.roll(top, step, 1)
            top = jnp.maximum(top, jnp.where((lane & step) == 0, up, down))
        tops.append(top)
    return jnp.concatenate(tops, axis=1)


def third_kernel(count, active_two, vectors, cot, slope_two, normal_two, scale_two, *rest):
    parts, (result, low_three, low_two, small, out) = rest[:count], rest[count:]
    put_out(parts, out)
    hidden = dot(active_two[...], out[...]) + vectors[6:7, 0:512]
    gain = vectors[7:8, 0:512]
    normal, scale, value = norm(hidden, gain, vectors[8:9, 0:512])
    ones = (
        lax.broadcasted_iota(jnp.int32, (128, 128), 0) // GROUP
        == lax.broadcasted_iota(jnp.int32, (128, 128), 1) // GROUP
    ).astype(F32).astype(BF)
    grown = jnp.exp(value - group_max(value))
    share = grown / group_sum(grown, ones)
    result[...] = share.astype(BF)
    weighed = cot[...].astype(F32) * share
    through = weighed - share * group_sum(weighed, ones)
    total = functools.partial(jnp.sum, axis=0, keepdims=True)
    small[3:4, 0:512] = total(through * normal)
    small[3:4, 512:1024] = total(through)
    scaled = through * gain
    first = jnp.mean(scaled, -1, keepdims=True)
    second = jnp.mean(scaled * normal, -1, keepdims=True)
    low = (scale * (scaled - first - normal * second)).astype(BF)
    low_three[...] = low
    small[4:5, 0:512] = total(low.astype(F32))
    small[4:5, 512:1024] = jnp.zeros((1, 512), F32)
    small[5:8, :] = jnp.zeros((3, 1024), F32)
    back = dot_t(low, out[...])
    low, *sums = norm_mish_back(back, slope_two[...], normal_two[...], scale_two[...], vectors[4:5, :])
    low_two[...] = low
    for k in range(3):
        small[k : k + 1, :] = sums[k]


def fourth_kernel(low_two, small_two, vectors, hid, slope_one, normal_one, scale_one, x, onehot, moves, *rest):
    low_one, *grads, small = rest
    back = dot_t(low_two[...], hid[...])
    low, *sums = norm_mish_back(back, slope_one[...], normal_one[...], scale_one[...], vectors[1:2, :])
    low_one[...] = low
    for k in range(3):
        small[86 + k : 87 + k, :] = sums[k]
    small[89:94, :] = small_two[0:5, :]
    small[94:96, :] = jnp.zeros((2, 1024), F32)
    small[0:80, :] = dot(onehot[...], low)
    small[80:86, :] = dot(moves[...], low)
    give_lat(x, low, small, grads)


def fifth_kernel(share, low_one, lat, active_two, low_three, own, beside, across, grad, held):
    held[...] = dot_t(low_one[...], lat[...]).astype(BF)
    for step, piece in enumerate((own, beside.at[0], across, beside.at[1])):
        start = at((lax.axis_index("mp") ^ step) * 128, 128)
        piece[0] = share[:, start]
        piece[1] = held[:, start]
    give_out(active_two, low_three, grad)


def sixth_kernel(active_one, low_two, grad):
    give_hid(active_one, low_two, grad)


def spots(c):
    x, y, z, core = place_of()
    for k in range(4):
        for far in range(4):
            yield k, far, 2 * (z ^ far) + (y ^ (k >> 1)), 2 * (x ^ (k & 1)) + (core ^ c)


def part_of(parts, c, k, far, quarter):
    half = quarter // 2 if k == 3 else 0
    return parts[len(parts) // 2 * c + k + half].at[4 * (quarter - 2 * half) + far]


def put_lat(parts, lat):
    if len(parts) == 1:
        lat[...] = parts[0][...]
        return
    for c in range(2):
        for k, far, i, j in spots(c):
            block = part_of(parts, c, k, far, 0)
            for h in range(2):
                lat[at(64 * i, 64, 64), at(256 * j + 128 * h, 128)] = block[64 * h : 64 * h + 64, :]


def put_hid(parts, hid):
    if len(parts) == 1:
        hid[...] = parts[0][...]
        return
    for c in range(2):
        for k, far, i, j in spots(c):
            for n in range(2):
                hid[at(256 * j + 128 * n, 128), at(128 * i, 128)] = part_of(parts, c, k, far, n + 1)[...]


def put_out(parts, out):
    if len(parts) == 1:
        out[...] = parts[0][...]
        return
    for c in range(2):
        for k, far, i, j in spots(c):
            out[at(128 * i, 128), at(128 * j, 128)] = part_of(parts, c, k, far, 3)[...]


def target(i, j):
    x, y, z, core = place_of()
    return core ^ (j & 1), 2 * (y ^ (i & 1)) + (x ^ (j >> 1)), z ^ (i >> 1)


def give_lat(rows, low, small, grads):
    if len(grads) == 2:
        grads[0][...] = t_dot(rows[...], low)
        grads[1][...] = small[...]
        return
    (grad,) = grads
    for j in range(4):
        for i in range(0, 8, 4):
            value = t_dot(rows[:, 64 * i : 64 * i + 256], low[:, 256 * j : 256 * j + 256]).astype(BF)
            for n in range(4):
                c, k, far = target(i + n, j)
                for h in range(2):
                    top = at(512 * k + 128 * far + 64 * h, 64, 64)
                    grad[c, top, :] = value[64 * n : 64 * n + 64, 128 * h : 128 * h + 128]
    for n in range(8):
        top = 2048 + 96 * (n % 4)
        grad[place_of()[3] ^ (n // 4), top : top + 96, :] = small[:, 128 * n : 128 * n + 128].astype(BF)


def give_hid(rows, low, grad):
    if len(grad.shape) == 2:
        grad[...] = t_dot(rows[...], low[...])
        return
    for j in range(4):
        for i in range(0, 8, 2):
            value = t_dot(rows[:, 256 * j : 256 * j + 256], low[:, 128 * i : 128 * i + 256]).astype(BF)
            for n in range(2):
                c, k, far = target(i + n, j)
                grad[c, k, far] = value[:, 128 * n : 128 * n + 128]


def give_out(rows, low, grad):
    if len(grad.shape) == 2:
        grad[...] = t_dot(rows[...], low[...])
        return
    for j in range(0, 4, 2):
        for i in range(0, 8, 2):
            value = t_dot(rows[:, 128 * i : 128 * i + 256], low[:, 128 * j : 128 * j + 256]).astype(BF)
            for m in range(2):
                for n in range(2):
                    c, k, far = target(i + n, j + m)
                    grad[c, k, far] = value[128 * n : 128 * n + 128, 128 * m : 128 * m + 128]


def plus(*values):
    return functools.reduce(lambda a, b: a + b, (v.astype(F32) for v in values))


def chunk_kernel(*rest):
    blocks, chunk = rest[:4], rest[4]
    for far, block in enumerate(blocks):
        for n in range(4):
            chunk[4 * n + far] = block[128 * n : 128 * n + 128, :]


def join_kernel(kept, came, own, by_x, by_y, cross_y, cross_x):
    for k, out in enumerate((own, by_x, by_y)):
        rows = slice(512 * k, 512 * k + 512)
        out[...] = kept[0, rows, :] + came[rows, :]
    for out, top, small in ((cross_y, 1536, 2048), (cross_x, 1792, 2240)):
        out[0:256, :] = kept[0, top : top + 256, :] + came[top : top + 256, :]
        out[256:448, :] = kept[0, small : small + 192, :] + came[small : small + 192, :]


def join_more_kernel(hid_kept, out_kept, hid_came, out_came, own, by_x, by_y, cross_y, cross_x):
    for far in range(4):
        top = 384 * far
        for k, out in enumerate((own, by_x, by_y)):
            out[top : top + 256, :] = hid_kept[0, k, far] + hid_came[k, far]
            out[top + 256 : top + 384, :] = out_kept[0, k, far] + out_came[k, far]
        out, top = (cross_y, cross_x)[far // 2], 384 * (far % 2)
        out[top : top + 256, :] = hid_kept[0, 3, far] + hid_came[3, far]
        out[top + 256 : top + 384, :] = out_kept[0, 3, far] + out_came[3, far]


def cross_kernel(by_x, by_y, cross_y, cross_x, from_y, from_x, to_x, to_y):
    rows = by_x.shape[0]
    half = rows // 2
    to_x[:half, :] = by_x[:half, :] + from_y[:half, :]
    to_x[half:rows, :] = by_x[half:, :]
    to_y[:half, :] = by_y[:half, :]
    to_y[half:rows, :] = by_y[half:, :] + from_x[:half, :]
    if to_x.shape[0] > rows:
        to_x[rows:, :] = cross_y[half:, :] + from_y[half:, :]
        to_y[rows:, :] = cross_x[half:, :] + from_x[half:, :]


def plane_kernel(own, to_x, to_y, from_x, from_y, kept, near, middle, far):
    size = kept.shape[0]
    for out, step in ((kept, 0), (near, 1), (middle, 2), (far, 3)):
        rows = slice(size * step, size * step + size)
        out[0:size, :] = plus(own[rows, :], from_x[rows, :], from_y[rows, :]).astype(out.dtype)
    if far.shape[0] > size:
        far[size : size + 192, :] = to_x[512:, :] + from_x[512:, :]
        far[size + 192 :, :] = to_y[512:, :] + from_y[512:, :]


def line_kernel(middle, far, came, to_middle):
    size = middle.shape[0]
    to_middle[0:size, :] = middle[...] + came[0:size, :]
    if far.shape[0] > size:
        to_middle[size:, :] = far[size:, :] + came[size:, :]


def small_kernel(to_middle, came, small):
    small[...] = to_middle[128:, :] + came[128:, :]


def pack_kernel(across, beside, both):
    both[0:2] = across[...]
    both[2:4] = beside[1]


def finish_kernel(*rest):
    (kept_a, near_a, middle_a, kept_b, near_b, middle_b), pieces, outs = rest[:6], rest[6:-5], rest[-5:]
    lat, hid, out, *features = outs

    def total(rows, chunk):
        return plus(*(ref[rows, :] for ref in chunk))

    first, second = (kept_a, near_a, middle_a), (kept_b, near_b, middle_b)
    lat[:, 0:128] = total(slice(0, 64), first)
    lat[:, 128:256] = total(slice(64, 128), first)
    hid[...] = total(slice(0, 256), second)
    out[...] = total(slice(256, 384), second)
    put_features(pieces, features)


def put_features(pieces, outs):
    own, beside, across = pieces
    rows = own.shape[1]
    for step, piece in enumerate((own, beside.at[0], across.at[0:2], across.at[2:4])):
        for k, out in enumerate(outs):
            out[at((lax.axis_index("mp") ^ step) * rows, rows), :] = piece[k]


def rows_kernel(*rest):
    put_features(rest[:-2], rest[-2:])


def last_kernel(count, *rest):
    parts, (table, task), outs, whole = rest[:count], rest[count : count + 2], rest[count + 2 : -1], rest[-1]
    if count == 1:
        whole[...] = parts[0][...]
    for c, part in enumerate(parts if count > 1 else ()):
        for n in range(4):
            column = at(128 * (4 * (place_of()[3] ^ c) + n), 128)
            whole[:, column] = part[96 * n : 96 * n + 96, :].astype(F32)
    table_grad, act_grad, task_grad, *vectors = outs
    by_task = whole[0:80, :].astype(BF)
    table_grad[...] = dot_t(by_task, task[...].astype(BF))
    task_grad[...] = t_dot(table[...].astype(BF), by_task)
    act_grad[...] = whole[80:86, :]
    for k in range(6):
        vectors[k][...] = whole[86 + k, :]
    vectors[6][...] = whole[93, 0:512]
    vectors[7][...] = whole[92, 0:512]
    vectors[8][...] = whole[92, 512:1024]


CORE, X, Y, NEAR, MIDDLE = 1, 2, 4, 8, 16


def after(value, *others):
    return lax.optimization_barrier((value, others))[0]


def gather_tree(block, pieces, before, swap):
    middle, near = swap(block, MIDDLE), swap(block, NEAR)
    line, before, pieces = lax.optimization_barrier(
        ((block, near, middle, swap(middle, NEAR)), before, trade(pieces, swap))
    )
    (chunk,) = call(chunk_kernel, [((16, 128, 128), BF)], *line)
    from_x, from_y = swap(chunk, X), swap(chunk, Y)
    other = swap(chunk, CORE)
    cross_x, cross_y = after((from_x[:8], from_y[8:]), other)
    own = [chunk, from_x, from_y, swap(cross_x, Y), swap(cross_y, X)]
    others = [other, *(swap(part, CORE) for part in own[1:])]
    return own + others, pieces, before


def trade(pieces, swap):
    own, beside, across = pieces
    beside = swap(beside, CORE)
    (both,) = call(pack_kernel, [((4, *across.shape[1:]), BF)], across, beside)
    return own, beside, swap(both, X)


def join_cores(kernel, rows, *args):
    more = rows // 2 + (192 if kernel is join_kernel else 0)
    return call(kernel, [((rows, 128), BF)] * 3 + [((more, 128), BF)] * 2, *args)


def reduce_plane(cost, joined, swap, *ready):
    own, by_x, by_y, cross_y, cross_x = joined
    more = (by_x.shape[0] // 2 + cross_y.shape[0], 128)
    to_x, to_y = call(
        cross_kernel, [(more, BF)] * 2,
        *after((by_x, by_y, cross_y, cross_x), *ready), swap(cross_y, Y), swap(cross_x, X), cost=cost,
    )
    return own, to_x, to_y


def plane_sums(cost, own, to_x, to_y, swap, *ready):
    size = own.shape[0] // 4
    block, more = ((size, 128), BF), ((size + 2 * (to_x.shape[0] - own.shape[0]), 128), BF)
    return call(
        plane_kernel, [((size, 128), F32), block, block, more],
        own, to_x, to_y, after(swap(to_x, X), *ready), swap(to_y, Y), cost=cost,
    )


def shards(
    mesh_shape, latent, action, task_ids, action_mask, cotangent, task_table, lat_weight, act_weight, task_weight,
    bias_one, gain_one, shift_one, hid_weight, bias_two, gain_two, shift_two, out_weight, bias_three, gain_three, shift_three,
):
    count = mesh_shape[0] * mesh_shape[1]
    mp = mesh_shape[1]
    rows = latent.shape[0] // mp
    def swap(value, mask):
        return lax.ppermute(value, AXES, [(n, n ^ mask) for n in range(count)])

    tree = mesh_shape == (8, 4)
    weights = (lat_weight, hid_weight, out_weight)
    small_args = (
        task_ids.reshape(1, -1), action.T, action_mask.T, task_table, act_weight, task_weight,
        *(v.reshape(1, -1) for v in (
            bias_one, gain_one, shift_one, bias_two, gain_two, shift_two, bias_three, gain_three, shift_three,
        )),
    )
    sources = (latent, cotangent, *weights) if tree else (latent, cotangent)
    features = [((2, rows, 128), BF), ((2, 2, rows, 128), BF), ((2, rows, 128), BF)]
    outs = call(
        functools.partial(prep_kernel, len(sources)),
        features + ([((512, 128), BF)] if tree else []),
        *sources,
        scratch=[pltpu.VMEM(v.shape, v.dtype) for v in sources] + [pltpu.SemaphoreType.DMA((len(sources),))],
        far=True,
    )
    pieces, blocks = outs[:3], outs[3:]
    before, onehot, moves, vectors = call(
        functools.partial(entry_kernel, len(small_args)),
        [((rows, 1024), F32), ((80, rows), BF), ((6, rows), BF), ((16, 1024), F32)],
        *small_args,
        scratch=[pltpu.VMEM(v.shape, v.dtype) for v in small_args] + [pltpu.SemaphoreType.DMA((len(small_args),))],
        far=True,
    )
    if tree:
        out_parts, pieces, before = gather_tree(*blocks, pieces, before, swap)
        hid_parts = out_parts
        lat_parts = [part for n, part in enumerate(out_parts) if n % 5 < 4]
    else:
        pieces = trade(pieces, swap)
        lat_parts, hid_parts, out_parts = [
            (lax.all_gather(lax.all_gather(w.astype(BF), down, axis=0, tiled=True), over, axis=1, tiled=True),)
            for w, (down, over) in zip(weights, (("dp", "mp"), ("mp", "dp"), ("dp", "mp")))
        ]
    wide = [((rows, 1024), BF), ((rows, 1024), F32), ((rows, 1024), F32), ((rows, 1), F32)]
    x, cot, lat, active_one, slope_one, normal_one, scale_one = call(
        functools.partial(first_kernel, len(lat_parts)),
        [((rows, 512), BF), ((rows, 512), BF), ((512, 1024), BF)] + wide,
        before, vectors, *lat_parts, *pieces,
    )
    hid, active_two, slope_two, normal_two, scale_two = call(
        second_kernel, [((1024, 1024), BF)] + wide, active_one, vectors, *hid_parts
    )
    if tree:
        sums = [((2, 2432, 128), BF)], ((2, 4, 4, 128, 128), BF), ((2, 4, 4, 256, 128), BF)
    else:
        sums = [((512, 1024), F32), ((SMALL, 1024), F32)], ((1024, 512), F32), ((1024, 1024), F32)
    share, low_three, low_two, small_two = call(
        functools.partial(third_kernel, len(out_parts)),
        [((rows, 512), BF), ((rows, 512), BF), ((rows, 1024), BF), ((8, 1024), F32)],
        active_two, vectors, cot, slope_two, normal_two, scale_two, *out_parts,
        scratch=[pltpu.VMEM((1024, 512), BF)],
    )
    low_one, *lat_sums = call(
        fourth_kernel, [((rows, 1024), BF)] + sums[0],
        low_two, small_two, vectors, hid, slope_one, normal_one, scale_one, x, onehot, moves,
        scratch=[pltpu.VMEM((SMALL, 1024), F32)],
    )
    *finals, out_sum = call(
        fifth_kernel, features + [sums[1]],
        share, low_one, lat, active_two, low_three,
        scratch=[pltpu.VMEM((rows, 512), BF)],
    )
    if tree:
        lat_came = after(swap(lat_sums[0][1], CORE), out_sum)
        first = join_cores(join_kernel, 512, lat_sums[0], lat_came)
        out_came = swap(out_sum[1], CORE)
        active_one = after(active_one, first, out_came)
    (hid_sum,) = call(sixth_kernel, [sums[2]], active_one, low_two)
    finals = trade(finals, swap)
    columns = [(latent.shape, BF)] * 2
    if tree:
        second = join_cores(join_more_kernel, 1536, hid_sum, out_sum, swap(hid_sum[1], CORE), out_came)
        first = reduce_plane(2, first, swap, second)
        second = reduce_plane(0, second, swap, first)
        *first, middle, far = plane_sums(0, *first, swap, second)
        (to_middle,) = call(line_kernel, [(far.shape, BF)], middle, far, swap(far, NEAR), cost=0.3)
        first += [swap(first[1], NEAR), swap(to_middle, MIDDLE)]
        *second, middle, far = plane_sums(0, *second, swap, to_middle)
        (small,) = call(small_kernel, [((384, 128), BF)], to_middle, after(first[-1], second))
        (to_middle,) = call(line_kernel, [(far.shape, BF)], middle, far, after(swap(far, NEAR), small))
        second += [swap(second[1], NEAR), swap(to_middle, MIDDLE)]
        parts = [small, after(swap(small, CORE), to_middle)]
        first, second = [(part[0], part[2], part[3]) for part in (first, second)]
        lat_grad, hid_grad, out_grad, result, latent_grad = call(
            finish_kernel, [(w.shape, F32) for w in weights] + columns, *first, *second, *finals
        )
    else:
        out_grad, hid_grad, lat_grad = [
            lax.psum_scatter(
                lax.psum_scatter(g, over, scatter_dimension=1, tiled=True), down, scatter_dimension=0, tiled=True
            )
            for g, (down, over) in zip((out_sum, hid_sum, lat_sums[0]), (("dp", "mp"), ("mp", "dp"), ("dp", "mp")))
        ]
        parts = [lax.psum(lat_sums[1], AXES)]
        result, latent_grad = call(rows_kernel, columns, *finals)
    table_grad, act_grad, task_grad, *vector_grads = call(
        functools.partial(last_kernel, len(parts)),
        [(task_table.shape, F32), (act_weight.shape, F32), (task_weight.shape, F32)]
        + [((1024,), F32)] * 6
        + [((512,), F32)] * 3,
        *parts, task_table, task_weight,
        scratch=[pltpu.VMEM((SMALL, 1024), F32)],
    )
    return (
        result, latent_grad, table_grad, lat_grad, act_grad, task_grad, *vector_grads[0:3], hid_grad, *vector_grads[3:6],
        out_grad, *vector_grads[6:9],
    )


def solution(mesh):
    both = P("dp", "mp")
    turned = P("mp", "dp")
    whole = P()
    return jax.shard_map(
        functools.partial(shards, (mesh.shape["dp"], mesh.shape["mp"])),
        mesh=mesh,
        in_specs=(
            both, P("dp", None), P("dp"), whole, both, whole, both, whole, whole, whole, whole, whole,
            turned, whole, whole, whole, both, whole, whole, whole,
        ),
        out_specs=(
            both, both, whole, both, whole, whole, whole, whole, whole, turned, whole, whole, whole, both,
            whole, whole, whole,
        ),
        check_vma=False,
    )
```
